32 devices in a mesh: parts: 32 (over z, y, x, core).
Axes of the slice: x: 2, y: 2, z: 4, core: 2. Of those that a mesh axis runs over, the one named last changes fastest.
Arguments:
- a_cols: int32 [1024, 7], replicated, may hold values from 0 to 1023, as said below
- p_col: int32 [1024], replicated, may hold values from 0 to 63, as said below
- coarse_cols: int32 [64, 14], replicated, may hold values from 0 to 63, as said below
- a_vals: bfloat16 [1024, 7, 192, 192], P('parts'), may hold values from -0.15625 to 0.15625
- p_vals: bfloat16 [1024, 192, 192], P('parts'), may hold values from -0.5 to 0.5
Outputs:
- coarse: float32 [64, 14, 192, 192], P('parts')
The draws below stay inside these ranges and needn't reach their ends.
Inputs may be any that keep to these rules, and one draw needn't show every extreme that they name: `a_cols`: regions are numbered 0 to 31; fine row i lies in region g = i // 32 with local index l = i % 32; o is the list 0, 1, -1, 4, -4, 16, -16 and region g + o(s) is taken cyclically. Slot 0 of row i holds i. For l < 6, slot l + 1 holds the row of region g + o(l + 1) whose local index is q - 1, where q is the slot whose offset is the negative of o(l + 1), and the other slots hold rows of region g with local index 6 or more. For l >= 6 slots 1 to 6 hold rows of region g. For fine row i of region g with local index l: if l < 6, p_col[i] is a coarse row of region g + o(l + 1), else of region g; coarse row r belongs to region r // 2. `coarse_cols`: row r of region g lists, in an order of its own, the 2 coarse rows of each of the regions g + o(s), s = 0 to 6.
All inputs are finite; a program needn't handle non-finite values.
Results may differ from the reference program's by a relative error of at most 0.0029.
Values may be sent and summed in bfloat16 or wider, within the bound.
A program may use at most 256 MiB of HBM per device.

```python
import jax
import jax.numpy as jnp
from jax import lax

B = 192
C = 192
KA = 7
RC = 2
RF = 32
NF = 1024
NC = 64
KC = 14


OFFSETS = [0, 1, -1, 4, -4, 16, -16]


OPPOSITE = [0, 2, 1, 4, 3, 6, 5]


def draw_a_cols(key, part):
    regions = NF // RF
    fine_rows = jnp.arange(NF, dtype=jnp.int32)
    region_of = fine_rows // RF
    local_row = fine_rows % RF
    key_any, key_inner = jax.random.split(key)
    any_rows = jax.random.randint(key_any, (NF, KA), 0, RF, dtype=jnp.int32)
    inner_rows = jax.random.randint(key_inner, (NF, KA), 6, RF, dtype=jnp.int32)
    slot_ids = jnp.arange(KA, dtype=jnp.int32)[None, :]
    offsets = jnp.array(OFFSETS, dtype=jnp.int32)
    opposite = jnp.array(OPPOSITE, dtype=jnp.int32)
    neighbour = (region_of[:, None] + offsets[None, :]) % regions * RF + (opposite[None, :] - 1)
    own_pick = region_of[:, None] * RF + jnp.where(local_row[:, None] < 6, inner_rows, any_rows)
    columns = jnp.where(slot_ids == 0, fine_rows[:, None], jnp.where(local_row[:, None] == slot_ids - 1, neighbour, own_pick))
    return columns.astype(jnp.int32)


def draw_p_col(key, part):
    regions = NF // RF
    fine_rows = jnp.arange(NF, dtype=jnp.int32)
    region_of = fine_rows // RF
    local_row = fine_rows % RF
    offsets = jnp.array(OFFSETS, dtype=jnp.int32)
    choose = jax.random.randint(key, (NF,), 0, RC, dtype=jnp.int32)
    shift_by = jnp.where(local_row < 6, offsets[jnp.minimum(local_row + 1, 6)], 0)
    return ((region_of + shift_by) % regions * RC + choose).astype(jnp.int32)


def draw_coarse_cols(key, part):
    regions = NC // RC
    coarse_rows = jnp.arange(NC, dtype=jnp.int32)
    region_of = coarse_rows // RC
    slot_ids = jnp.arange(KC, dtype=jnp.int32)
    offsets = jnp.array(OFFSETS, dtype=jnp.int32)
    base = (region_of[:, None] + offsets[slot_ids // RC][None, :]) % regions * RC + (slot_ids % RC)[None, :]
    orders = jax.vmap(lambda row_key: jax.random.permutation(row_key, KC))(jax.random.split(key, NC))
    return jnp.take_along_axis(base, orders.astype(jnp.int32), axis=1).astype(jnp.int32)


def shard_levels(own_key, shape, pieces, smallest, top_value):
    loudness = 1.0
    for position, shards_of in pieces:
        draws = jax.random.uniform(jax.random.fold_in(jax.random.fold_in(own_key, 6), position), (shards_of,), jnp.float32, smallest / len(pieces), top_value / len(pieces))
        loudness = loudness * jnp.repeat(jnp.exp(draws), shape[position] // shards_of).reshape((-1,) + (1,) * (len(shape) - 1 - position))
    return loudness


def scatter_about(rng, extent, width, most, cuts=(), kind=jnp.bfloat16):
    drawn = jax.random.normal(rng, extent, jnp.float32) * width
    if len(cuts) > 0:
        drawn = shard_levels(rng, extent, cuts, -0.22, 0.18) * drawn
    return jnp.clip(drawn, min=-most, max=most).astype(kind)


def setup_inputs(seed: int = 0) -> dict:
    key_of = jax.random.split(jax.random.key(seed), 6)
    return {
        "a_cols": draw_a_cols(jax.random.fold_in(key_of[5], 71), 0),
        "p_col": draw_p_col(jax.random.fold_in(key_of[5], 71), 0),
        "coarse_cols": draw_coarse_cols(jax.random.fold_in(key_of[5], 71), 0),
        "a_vals": scatter_about(key_of[3], (NF, KA, B, B), (KA * B) ** -0.5, 0.15625, ((0, 32),)),
        "p_vals": scatter_about(key_of[4], (NF, B, C), 128 ** -0.5, 0.5, ((0, 32),)),
    }


def reference(a_cols, p_col, coarse_cols, a_vals, p_vals):
    regions = NF // RF

    def region_step(region_id, accumulated):
        first_row = (jnp.asarray(region_id) * RF).astype(jnp.int32)
        columns = lax.dynamic_slice_in_dim(a_cols, first_row, RF, 0)
        blocks = lax.dynamic_slice_in_dim(a_vals, first_row, RF, 0).astype(jnp.float32)
        own_prolong = lax.dynamic_slice_in_dim(p_vals, first_row, RF, 0).astype(jnp.float32)
        gathered = p_vals[columns].astype(jnp.float32)
        products = jnp.einsum('ikab,ikbc->ikac', blocks, gathered).astype(jnp.bfloat16)
        galerkin = jnp.einsum('iba,ikbc->ikac', own_prolong, products.astype(jnp.float32))
        targets = p_col[columns]
        coarse_rows = lax.dynamic_slice_in_dim(p_col, first_row, RF, 0)
        listed = coarse_cols[coarse_rows]
        equal_slots = listed[:, None, :] == targets[:, :, None]
        first_slot = equal_slots & (jnp.cumsum(equal_slots.astype(jnp.int32), axis=2) == 1)
        placed = jnp.einsum('ikm,ikab->imab', first_slot.astype(jnp.float32), galerkin,
                            precision=lax.Precision.HIGHEST)
        return accumulated.at[coarse_rows].add(placed)

    return lax.fori_loop(0, regions, region_step, jnp.zeros((NC, KC, C, C), jnp.float32))
```

```python
import functools

import jax
import jax.numpy as jnp
from jax import lax
from jax.experimental import pallas as pl
from jax.experimental.pallas import tpu as pltpu
from jax.sharding import PartitionSpec as P

OFFSETS = [0, 1, -1, 4, -4, 16, -16]
OPPOSITE = [0, 2, 1, 4, 3, 6, 5]
KA = 7
FACES = 6
VMEM_LIMIT = 48 * 1024 * 1024
F32 = jnp.float32
BF16 = jnp.bfloat16


def dot(left, right):
    return jnp.dot(left, right, preferred_element_type=F32)


def pack(out_ref, at, blocks):
    for n, block in enumerate(blocks):
        out_ref[at + (n,)] = block[:, :128].astype(BF16)
    for n in range(2):
        rest = jnp.concatenate([blocks[2 * n][:, 128:], blocks[2 * n + 1][:, 128:]], axis=1)
        out_ref[at + (4 + n,)] = rest.astype(BF16)


def face_kernel(rows, row_count, earlier, cols_ref, pcol_ref, a_hbm, p_hbm, *rest):
    outs, (a_buf, p_buf, sums, a_sem, p_sem) = rest[earlier:-5], rest[-5:]
    region = lax.axis_index("parts")
    first_row = region * row_count
    copies = {}
    for n, row in enumerate(rows):
        for k in range(KA):
            copy = pltpu.make_async_copy(a_hbm.at[row, k], a_buf.at[n, k], a_sem.at[n, k])
            copy.start()
            if k == row + 1:
                copies[n, k] = (copy,)
                continue
            column = row if k == 0 else cols_ref[k, first_row + row] - first_row
            other = pltpu.make_async_copy(p_hbm.at[column], p_buf.at[n, k], p_sem.at[n, k])
            other.start()
            copies[n, k] = (copy, other)
    for n, row in enumerate(rows):
        for copy in copies[n, 0]:
            copy.wait()
        own_t = p_buf[n, 0].T
        diagonal = dot(own_t, dot(a_buf[n, 0], p_buf[n, 0]).astype(BF16))
        copies[n, row + 1][0].wait()
        half = dot(own_t, a_buf[n, row + 1])
        sums[...] = jnp.zeros_like(sums)
        for k in range(1, KA):
            if k == row + 1:
                continue
            for copy in copies[n, k]:
                copy.wait()
            side = pcol_ref[cols_ref[k, first_row + row]] % 2
            sums[side] += dot(a_buf[n, k], p_buf[n, k])
        inner = [dot(own_t, sums[c].astype(BF16)) for c in range(2)]
        out_ref, at = (outs[0], (n,)) if len(outs) == 1 else (outs[n], ())
        pack(out_ref, at, [diagonal, inner[0], inner[1], half])


def face_terms(rows, merged, a_t, p_col, a_vals, p_vals, earlier):
    row_count, _, width, _ = a_vals.shape
    one = jax.ShapeDtypeStruct((6, width, 128), BF16)
    both = jax.ShapeDtypeStruct((2, 6, width, 128), BF16)
    smem = pl.BlockSpec(memory_space=pltpu.SMEM)
    vmem = pl.BlockSpec(memory_space=pltpu.VMEM)
    anyw = pl.BlockSpec(memory_space=pl.ANY)
    return pl.pallas_call(
        functools.partial(face_kernel, rows, row_count, len(earlier)),
        out_shape=[both] if merged else [one, one],
        in_specs=[smem, smem, anyw, anyw] + [anyw] * len(earlier),
        out_specs=[vmem] * (1 if merged else 2),
        scratch_shapes=[
            pltpu.VMEM((2, KA, width, width), BF16),
            pltpu.VMEM((2, KA, width, width), BF16),
            pltpu.VMEM((2, width, width), F32),
            pltpu.SemaphoreType.DMA((2, KA)),
            pltpu.SemaphoreType.DMA((2, KA)),
        ],
        compiler_params=pltpu.CompilerParams(vmem_limit_bytes=VMEM_LIMIT),
        cost_estimate=pl.CostEstimate(flops=24 * 2 * width**3, bytes_accessed=5_000_000, transcendentals=0),
        name="faces_%d" % rows[0],
    )(a_t, p_col, a_vals, p_vals, *earlier)


def slot_of(listed_ref, coarse_row, local, column):
    slots = listed_ref.shape[0]
    found = jnp.int32(0)
    for m in reversed(range(slots)):
        found = jnp.where(listed_ref[m, coarse_row] == column, jnp.int32(m), found)
    return local * slots + found


def inner_kernel(row_count, coarse_count, pair, cols_ref, pcol_ref, listed_ref, a_ref, p_ref, out_ref, table):
    step = pl.program_id(0)
    region = lax.axis_index("parts")
    first_row = region * row_count
    first_coarse = region * coarse_count
    slots = listed_ref.shape[0]

    @pl.when(step == 0)
    def _():
        out_ref[...] = jnp.zeros_like(out_ref)
        for r in range(coarse_count):
            for m in reversed(range(slots)):
                table[r, listed_ref[m, first_coarse + r]] = r * slots + m

    for n in range(pair):
        row = FACES + step * pair + n
        local = pcol_ref[first_row + row] - first_coarse
        own_t = p_ref[row].T
        columns = [cols_ref[k, first_row + row] for k in range(KA)]
        products = [dot(a_ref[n, k], p_ref[columns[k] - first_row]).astype(BF16) for k in range(KA)]
        for k in range(KA):
            target = table[local, pcol_ref[columns[k]]]
            out_ref[target] += dot(own_t, products[k])


def inner_terms(a_t, p_col, listed_t, a_vals, p_vals, coarse_count):
    row_count, _, width, _ = a_vals.shape
    slots, coarse_all = listed_t.shape
    pair = 2
    smem = pl.BlockSpec(memory_space=pltpu.SMEM)
    return pl.pallas_call(
        functools.partial(inner_kernel, row_count, coarse_count, pair),
        out_shape=jax.ShapeDtypeStruct((coarse_count * slots, width, width), F32),
        grid=((row_count - FACES) // pair,),
        in_specs=[
            smem,
            smem,
            smem,
            pl.BlockSpec((pair, KA, width, width), lambda s: (s + FACES // pair, 0, 0, 0)),
            pl.BlockSpec((row_count, width, width), lambda s: (0, 0, 0), pipeline_mode=pl.Buffered(1)),
        ],
        out_specs=pl.BlockSpec((coarse_count * slots, width, width), lambda s: (0, 0, 0)),
        scratch_shapes=[pltpu.SMEM((coarse_count, coarse_all), jnp.int32)],
        compiler_params=pltpu.CompilerParams(vmem_limit_bytes=VMEM_LIMIT),
        cost_estimate=pl.CostEstimate(flops=364 * 4 * width**3, bytes_accessed=60_000_000, transcendentals=0),
        name="inner",
    )(a_t, p_col, listed_t, a_vals, p_vals)


def outer_kernel(row_count, coarse_count, regions, merged, pcol_ref, listed_ref, *rest):
    received, (p_ref, part_ref, out_ref) = rest[:-3], rest[-3:]
    region = lax.axis_index("parts")
    first_coarse = region * coarse_count
    out_ref[...] = part_ref[...]
    for face in range(FACES):
        ref, at = (received[4], (face - 4,)) if merged and face >= 4 else (received[face], ())
        sender = lax.rem(region - OFFSETS[face + 1] + regions, regions)
        coarse_row = pcol_ref[sender * row_count + face]
        local = coarse_row - first_coarse
        mine = OPPOSITE[face + 1] - 1
        own_row = region * coarse_count + local
        where = functools.partial(slot_of, listed_ref, own_row, local)
        for n, column in enumerate([coarse_row, sender * coarse_count, sender * coarse_count + 1]):
            target = where(column)
            out_ref[target, :, :128] += ref[at + (n,)].astype(F32)
            start = 64 * (n % 2)
            out_ref[target, :, 128:] += ref[at + (4 + n // 2,)][:, start : start + 64].astype(F32)
        block = dot(ref[at + (3,)], p_ref[mine, :128]) + dot(ref[at + (5,)][:, 64:], p_ref[mine, 128:])
        out_ref[where(pcol_ref[region * row_count + mine])] += block


def outer_terms(p_col, listed_t, received, p_vals, part, coarse_count, regions, merged):
    row_count, width, _ = p_vals.shape
    smem = pl.BlockSpec(memory_space=pltpu.SMEM)
    vmem = pl.BlockSpec(memory_space=pltpu.VMEM)
    faces = pl.BlockSpec((FACES, width, width), lambda s: (0, 0, 0))
    whole = pl.BlockSpec(part.shape, lambda s: (0, 0, 0))
    return pl.pallas_call(
        functools.partial(outer_kernel, row_count, coarse_count, regions, merged),
        out_shape=jax.ShapeDtypeStruct(part.shape, F32),
        grid=(1,),
        in_specs=[smem, smem] + [vmem] * len(received) + [faces, whole],
        out_specs=whole,
        compiler_params=pltpu.CompilerParams(vmem_limit_bytes=VMEM_LIMIT),
        name="outer",
    )(p_col, listed_t, *received, p_vals, part)


def per_device(a_cols, p_col, coarse_cols, a_vals, p_vals):
    regions = lax.axis_size("parts")
    coarse_count = coarse_cols.shape[0] // regions
    a_t = a_cols.T
    listed_t = coarse_cols.T
    merged = (OFFSETS[5] - OFFSETS[6]) % regions == 0
    sent = [None] * FACES
    outs = []
    for first in (4, 2, 0):
        outs = face_terms((first, first + 1), merged and first == 4, a_t, p_col, a_vals, p_vals, outs)
        for n, out in enumerate(outs):
            by = OFFSETS[first + n + 1]
            sent[first + n] = lax.ppermute(out, "parts", [(i, (i + by) % regions) for i in range(regions)])
    received = [value for value in sent if value is not None]
    part = inner_terms(a_t, p_col, listed_t, a_vals, p_vals, coarse_count)
    out = outer_terms(p_col, listed_t, received, p_vals, part, coarse_count, regions, merged)
    return out.reshape((coarse_count, -1) + out.shape[1:])


def solution(mesh):
    placed = (P(), P(), P(), P("parts", None, None, None), P("parts", None, None))
    return jax.shard_map(
        per_device,
        mesh=mesh,
        in_specs=placed,
        out_specs=P("parts", None, None, None),
        check_vma=False,
    )
```

```python
import functools

import jax
import jax.numpy as jnp
from jax import lax
from jax.experimental import pallas as pl
from jax.experimental.pallas import tpu as pltpu
from jax.sharding import PartitionSpec as P

OFFSETS = [0, 1, -1, 4, -4, 16, -16]
OPPOSITE = [0, 2, 1, 4, 3, 6, 5]
KA = 7
FACES = 6
VMEM_LIMIT = 48 * 1024 * 1024
F32 = jnp.float32
BF16 = jnp.bfloat16


def dot(left, right):
    return jnp.dot(left, right, preferred_element_type=F32)


def pack(out_ref, at, blocks):
    for n, block in enumerate(blocks):
        out_ref[at + (n,)] = block[:, :128].astype(BF16)
    for n in range(2):
        rest = jnp.concatenate([blocks[2 * n][:, 128:], blocks[2 * n + 1][:, 128:]], axis=1)
        out_ref[at + (4 + n,)] = rest.astype(BF16)


def face_kernel(rows, row_count, earlier, cols_ref, pcol_ref, a_hbm, p_hbm, *rest):
    outs, (a_buf, p_buf, a_sem, p_sem) = rest[earlier:-4], rest[-4:]
    region = lax.axis_index("parts")
    first_row = region * row_count
    copies = {}
    for n, row in enumerate(rows):
        for k in range(KA):
            copy = pltpu.make_async_copy(a_hbm.at[row, k], a_buf.at[n, k], a_sem.at[n, k])
            copy.start()
            if k == row + 1:
                copies[n, k] = (copy,)
                continue
            column = row if k == 0 else cols_ref[k, first_row + row] - first_row
            other = pltpu.make_async_copy(p_hbm.at[column], p_buf.at[n, k], p_sem.at[n, k])
            other.start()
            copies[n, k] = (copy, other)
    for n, row in enumerate(rows):
        inner_slots = [k for k in range(1, KA) if k != row + 1]
        for k in range(KA):
            for copy in copies[n, k]:
                copy.wait()
        own_t = p_buf[n, 0].T
        half = dot(own_t, a_buf[n, row + 1])
        first = dot(a_buf[n, 0], p_buf[n, 0]).astype(BF16)
        sums = [None, None]
        for k in inner_slots:
            side = pcol_ref[cols_ref[k, first_row + row]] % 2
            product = dot(a_buf[n, k], p_buf[n, k])
            for c in range(2):
                part = jnp.where(side == c, product, 0.0)
                sums[c] = part if sums[c] is None else sums[c] + part
        diagonal = dot(own_t, first)
        inner = [dot(own_t, sums[c].astype(BF16)) for c in range(2)]
        out_ref, at = (outs[0], (n,)) if len(outs) == 1 else (outs[n], ())
        pack(out_ref, at, [diagonal, inner[0], inner[1], half])


def face_terms(rows, merged, a_t, p_col, a_vals, p_vals, earlier):
    row_count, _, width, _ = a_vals.shape
    one = jax.ShapeDtypeStruct((6, width, 128), BF16)
    both = jax.ShapeDtypeStruct((2, 6, width, 128), BF16)
    smem = pl.BlockSpec(memory_space=pltpu.SMEM)
    vmem = pl.BlockSpec(memory_space=pltpu.VMEM)
    anyw = pl.BlockSpec(memory_space=pl.ANY)
    hbm = pl.BlockSpec(memory_space=pltpu.HBM)
    return pl.pallas_call(
        functools.partial(face_kernel, rows, row_count, len(earlier)),
        out_shape=[both] if merged else [one, one],
        in_specs=[smem, smem, hbm, hbm] + [anyw] * len(earlier),
        out_specs=[vmem] * (1 if merged else 2),
        scratch_shapes=[
            pltpu.VMEM((2, KA, width, width), BF16),
            pltpu.VMEM((2, KA, width, width), BF16),
            pltpu.SemaphoreType.DMA((2, KA)),
            pltpu.SemaphoreType.DMA((2, KA)),
        ],
        compiler_params=pltpu.CompilerParams(vmem_limit_bytes=VMEM_LIMIT),
        cost_estimate=pl.CostEstimate(flops=24 * 2 * width**3, bytes_accessed=5_000_000, transcendentals=0),
        name="faces_%d" % rows[0],
    )(a_t, p_col, a_vals, p_vals, *earlier)


def slot_of(listed_ref, coarse_row, local, column):
    slots = listed_ref.shape[0]
    found = jnp.int32(0)
    for m in reversed(range(slots)):
        found = jnp.where(listed_ref[m, coarse_row] == column, jnp.int32(m), found)
    return local * slots + found


def inner_kernel(row_count, coarse_count, pair, cols_ref, pcol_ref, listed_ref, a_ref, p_ref, out_ref, table):
    step = pl.program_id(0)
    region = lax.axis_index("parts")
    first_row = region * row_count
    first_coarse = region * coarse_count
    slots = listed_ref.shape[0]

    @pl.when(step == 0)
    def _():
        out_ref[...] = jnp.zeros_like(out_ref)
        for r in range(coarse_count):
            for m in reversed(range(slots)):
                table[r, listed_ref[m, first_coarse + r]] = r * slots + m

    for n in range(pair):
        row = FACES + step * pair + n
        local = pcol_ref[first_row + row] - first_coarse
        own_t = p_ref[row].T
        columns = [cols_ref[k, first_row + row] for k in range(KA)]
        products = [dot(a_ref[n, k], p_ref[columns[k] - first_row]).astype(BF16) for k in range(KA)]
        for k in range(KA):
            target = table[local, pcol_ref[columns[k]]]
            out_ref[target] += dot(own_t, products[k])


def inner_terms(a_t, p_col, listed_t, a_vals, p_vals, coarse_count):
    row_count, _, width, _ = a_vals.shape
    slots, coarse_all = listed_t.shape
    pair = 2
    smem = pl.BlockSpec(memory_space=pltpu.SMEM)
    return pl.pallas_call(
        functools.partial(inner_kernel, row_count, coarse_count, pair),
        out_shape=jax.ShapeDtypeStruct((coarse_count * slots, width, width), F32),
        grid=((row_count - FACES) // pair,),
        in_specs=[
            smem,
            smem,
            smem,
            pl.BlockSpec((pair, KA, width, width), lambda s: (s + FACES // pair, 0, 0, 0)),
            pl.BlockSpec((row_count, width, width), lambda s: (0, 0, 0), pipeline_mode=pl.Buffered(1)),
        ],
        out_specs=pl.BlockSpec((coarse_count * slots, width, width), lambda s: (0, 0, 0)),
        scratch_shapes=[pltpu.SMEM((coarse_count, coarse_all), jnp.int32)],
        compiler_params=pltpu.CompilerParams(vmem_limit_bytes=VMEM_LIMIT),
        cost_estimate=pl.CostEstimate(flops=364 * 4 * width**3, bytes_accessed=60_000_000, transcendentals=0),
        name="inner",
    )(a_t, p_col, listed_t, a_vals, p_vals)


def outer_kernel(row_count, coarse_count, regions, merged, pcol_ref, listed_ref, *rest):
    received, (p_ref, part_ref, out_ref) = rest[:-3], rest[-3:]
    region = lax.axis_index("parts")
    first_coarse = region * coarse_count
    out_ref[...] = part_ref[...]
    for face in range(FACES):
        ref, at = (received[4], (face - 4,)) if merged and face >= 4 else (received[face], ())
        sender = lax.rem(region - OFFSETS[face + 1] + regions, regions)
        coarse_row = pcol_ref[sender * row_count + face]
        local = coarse_row - first_coarse
        mine = OPPOSITE[face + 1] - 1
        own_row = region * coarse_count + local
        where = functools.partial(slot_of, listed_ref, own_row, local)
        for n, column in enumerate([coarse_row, sender * coarse_count, sender * coarse_count + 1]):
            target = where(column)
            out_ref[target, :, :128] += ref[at + (n,)].astype(F32)
            start = 64 * (n % 2)
            out_ref[target, :, 128:] += ref[at + (4 + n // 2,)][:, start : start + 64].astype(F32)
        block = dot(ref[at + (3,)], p_ref[mine, :128]) + dot(ref[at + (5,)][:, 64:], p_ref[mine, 128:])
        out_ref[where(pcol_ref[region * row_count + mine])] += block


def outer_terms(p_col, listed_t, received, p_vals, part, coarse_count, regions, merged):
    row_count, width, _ = p_vals.shape
    smem = pl.BlockSpec(memory_space=pltpu.SMEM)
    vmem = pl.BlockSpec(memory_space=pltpu.VMEM)
    faces = pl.BlockSpec((FACES, width, width), lambda s: (0, 0, 0))
    whole = pl.BlockSpec(part.shape, lambda s: (0, 0, 0))
    return pl.pallas_call(
        functools.partial(outer_kernel, row_count, coarse_count, regions, merged),
        out_shape=jax.ShapeDtypeStruct(part.shape, F32),
        grid=(1,),
        in_specs=[smem, smem] + [vmem] * len(received) + [faces, whole],
        out_specs=whole,
        compiler_params=pltpu.CompilerParams(vmem_limit_bytes=VMEM_LIMIT),
        name="outer",
    )(p_col, listed_t, *received, p_vals, part)


def per_device(a_cols, p_col, coarse_cols, a_vals, p_vals):
    regions = lax.axis_size("parts")
    coarse_count = coarse_cols.shape[0] // regions
    a_t = a_cols.T
    listed_t = coarse_cols.T
    merged = (OFFSETS[5] - OFFSETS[6]) % regions == 0
    sent = [None] * FACES
    outs = []
    for first in (4, 2, 0):
        outs = face_terms((first, first + 1), merged and first == 4, a_t, p_col, a_vals, p_vals, outs)
        for n, out in enumerate(outs):
            by = OFFSETS[first + n + 1]
            sent[first + n] = lax.ppermute(out, "parts", [(i, (i + by) % regions) for i in range(regions)])
    received = [value for value in sent if value is not None]
    part = inner_terms(a_t, p_col, listed_t, a_vals, p_vals, coarse_count)
    out = outer_terms(p_col, listed_t, received, p_vals, part, coarse_count, regions, merged)
    return out.reshape((coarse_count, -1) + out.shape[1:])


def solution(mesh):
    placed = (P(), P(), P(), P("parts", None, None, None), P("parts", None, None))
    return jax.shard_map(
        per_device,
        mesh=mesh,
        in_specs=placed,
        out_specs=P("parts", None, None, None),
        check_vma=False,
    )
```
